32 devices in a mesh: term: 4 (over x, core), sec: 8 (over z, y).
Axes of the slice: x: 2, y: 2, z: 4, core: 2. Of those that a mesh axis runs over, the one named last changes fastest.
Arguments:
- psi_tiles: bfloat16 [192, 512, 512], P('sec'), may hold values from -6 to 6
- sectors: int32 [192, 2], P('sec'), may hold values from 0 to 15
- sources: int32 [4, 192], P('term', 'sec'), may hold values from 0 to 191, as said below
- left_env: bfloat16 [4, 16, 512, 512], P('term', None, 'sec'), may hold values from -0.25 to 0.25
- right_env: bfloat16 [4, 16, 512, 512], P('term', None, 'sec'), may hold values from -0.25 to 0.25
Outputs:
- applied: bfloat16 [192, 512, 512], P('sec', 'term')
The draws below stay inside these ranges and needn't reach their ends.
Inputs may be any that keep to these rules, and one draw needn't show every extreme that they name: sources[t, k] lies in the same aligned block of 24 tiles as k, and each row maps each such block one to one onto itself.
All inputs are finite; a program needn't handle non-finite values.
Results may differ from the reference program's by a relative error of at most 0.013.
Values may be sent and summed in bfloat16 or wider, within the bound.
A program may use at most 192 MiB of HBM per device.

```python
import jax
import jax.numpy as jnp

BLK = 512
NSEC = 16
TPD = 24
TILES = 192
TERMS = 4


def draw_sources(key, part):
    blocks = TILES // TPD
    keys = jax.random.split(key, TERMS * blocks)
    perms = jax.vmap(lambda one_key: jax.random.permutation(one_key, TPD))(keys)
    perms = perms.reshape(TERMS, blocks, TPD).astype(jnp.int32)
    offsets = (jnp.arange(blocks, dtype=jnp.int32) * TPD)[None, :, None]
    return (perms + offsets).reshape(TERMS, TILES).astype(jnp.int32)


def with_ends(entries, key, low, largest):
    spot = [jax.random.randint(jax.random.fold_in(key, axis), (), 0, length) for axis, length in enumerate(entries.shape)]
    widest = entries.shape.index(max(entries.shape))
    next_to = spot[:widest] + [(spot[widest] + 1) % entries.shape[widest]] + spot[widest + 1:]
    return entries.at[tuple(spot)].set(low).at[tuple(next_to)].set(largest)


def levels(key, extent, pieces, smallest, high):
    level, own = 1.0, jax.random.fold_in(key, 6)
    for axis_at, parts in pieces:
        draws = jnp.exp(jax.random.uniform(jax.random.fold_in(own, axis_at), (parts,), jnp.float32, smallest / len(pieces), high / len(pieces)))
        level = level * jnp.repeat(draws, extent[axis_at] // parts).reshape([-1 if axis == axis_at else 1 for axis in range(len(extent))])
    return level


def gaussian(key, shape, width, reach, cuts=(), kind=jnp.bfloat16):
    array = jax.random.normal(key, shape, jnp.float32) * width
    if len(cuts) > 0:
        array = levels(key, shape, cuts, -0.22, 0.18) * array
    return jnp.clip(array, min=-reach, max=reach).astype(kind)


def setup_inputs(seed: int = 0) -> dict:
    arg_keys = jax.random.split(jax.random.key(seed), 6)
    psi_tiles = gaussian(arg_keys[0], (TILES, BLK, BLK), 1.0, 6.0, ((0, 8),))
    sectors = with_ends(jax.random.randint(arg_keys[1], (TILES, 2), 0, NSEC), jax.random.fold_in(arg_keys[1], 1), 0, NSEC - 1).astype(jnp.int32)
    sources = draw_sources(jax.random.fold_in(arg_keys[5], 71), 0)
    left_env = gaussian(arg_keys[3], (TERMS, NSEC, BLK, BLK), BLK ** -0.5, 0.25, ((0, 4), (2, 8)))
    right_env = gaussian(arg_keys[4], (TERMS, NSEC, BLK, BLK), BLK ** -0.5, 0.25, ((0, 4), (2, 8)))
    return dict(psi_tiles=psi_tiles, sectors=sectors, sources=sources, left_env=left_env, right_env=right_env)


def reference(psi_tiles, sectors, sources, left_env, right_env):
    total = jnp.zeros((TILES, BLK, BLK), jnp.float32)
    for term in range(TERMS):
        moved = psi_tiles[sources[term]]
        right_sel = right_env[term][sectors[:, 1]]
        half = jnp.einsum("kij,kjl->kil", moved.astype(jnp.float32), right_sel.astype(jnp.float32)).astype(jnp.bfloat16)
        left_sel = left_env[term][sectors[:, 0]]
        term_out = jnp.einsum("kij,kjl->kil", left_sel.astype(jnp.float32), half.astype(jnp.float32)).astype(jnp.bfloat16)
        total = total + term_out.astype(jnp.float32)
    return total.astype(jnp.bfloat16)
```

```python
import functools

import jax
import jax.numpy as jnp
from jax import lax
from jax.experimental import pallas as pl
from jax.experimental.pallas import tpu as pltpu
from jax.sharding import PartitionSpec as P

MESH = pl.DeviceIdType.MESH
GROUPS = 4


def kernel(
    n,
    terms,
    sectors,
    sources,
    psi_h,
    left_h,
    right_h,
    out_h,
    psi_v,
    right_v,
    left_v,
    left_now,
    half_v,
    core_in,
    chip_in,
    local_sem,
    recv_sem,
    pair_sem,
    up_sem,
    down_sem,
    core_send,
    core_recv,
    chip_send,
    chip_recv,
    out_sem,
):
    tiles = psi_h.shape[0]
    rows = right_h.shape[1]
    line = n // 2
    wide = 2 * rows
    per_owner = line // terms
    size = tiles // GROUPS
    term = lax.axis_index("term")
    sec = lax.axis_index("sec")
    core = lax.rem(term, 2)
    chip = term // 2
    spot = sec // 2
    side = lax.rem(sec, 2)
    pair = spot * 2 + 1 - side
    other_core = chip * 2 + 1 - core
    other_chip = (1 - chip) * 2 + core
    has_up = spot + 1 < line
    has_down = spot > 0
    gathered = (right_v, left_v)
    owned = (right_h, left_h)

    def slot_of(place, parity):
        return place * 2 + parity

    def window(kind, slot):
        return gathered[kind].at[:, pl.ds(pl.multiple_of(slot * rows, rows), rows), :]

    def env_copy(kind, slot, src, target, sem):
        return pltpu.make_async_remote_copy(
            src_ref=src,
            dst_ref=window(kind, slot),
            send_sem=sem,
            recv_sem=recv_sem.at[kind, slot],
            device_id={"sec": target},
            device_id_type=MESH,
        )

    def to_pair(kind, place, src):
        return env_copy(kind, slot_of(place, side), src, pair, pair_sem.at[kind, place])

    def to_up(kind, place, src):
        return env_copy(kind, slot_of(place, side), src, sec + 2, up_sem.at[kind, place])

    def to_down(kind, place, src):
        return env_copy(kind, slot_of(place, side), src, sec - 2, down_sem.at[kind, place])

    def await_slot(kind, slot):
        env_copy(kind, slot, owned[kind], pair, pair_sem.at[kind, 0]).wait_recv()

    def push_own(kind):
        @pl.when(has_down)
        def _():
            to_down(kind, spot, owned[kind]).start()

        @pl.when(has_up)
        def _():
            to_up(kind, spot, owned[kind]).start()

        to_pair(kind, spot, owned[kind]).start()

    def forward(kind, step):
        @pl.when(spot - step >= 0)
        def _():
            place = spot - step
            slot = slot_of(place, side)
            await_slot(kind, slot)

            @pl.when(has_up)
            def _():
                to_up(kind, place, window(kind, slot)).start()

            to_pair(kind, place, window(kind, slot)).start()

        @pl.when(spot + step < line)
        def _():
            place = spot + step
            slot = slot_of(place, side)
            await_slot(kind, slot)

            @pl.when(has_down)
            def _():
                to_down(kind, place, window(kind, slot)).start()

            to_pair(kind, place, window(kind, slot)).start()

    def block_rows(block):
        return pl.ds(pl.multiple_of(block * wide, wide), wide)

    def group_rows(group):
        return pl.ds(group * size, size)

    def core_copy(block, group):
        owner = block // per_owner
        slot = (owner // 2) * per_owner + lax.rem(block, per_owner)
        return pltpu.make_async_remote_copy(
            src_ref=psi_v.at[group_rows(group), block_rows(block), :],
            dst_ref=core_in.at[slot, group_rows(group)],
            send_sem=core_send.at[block, group],
            recv_sem=core_recv.at[block, group],
            device_id={"term": other_core},
            device_id_type=MESH,
        )

    def chip_copy(block, group):
        return pltpu.make_async_remote_copy(
            src_ref=psi_v.at[group_rows(group), block_rows(block), :],
            dst_ref=chip_in.at[lax.rem(block, per_owner), group_rows(group)],
            send_sem=chip_send.at[block, group],
            recv_sem=chip_recv.at[block, group],
            device_id={"term": other_chip},
            device_id_type=MESH,
        )

    barrier = pltpu.get_barrier_semaphore()
    pl.semaphore_signal(barrier, inc=1, device_id={"sec": pair}, device_id_type=MESH)
    pl.semaphore_signal(barrier, inc=1, device_id={"term": other_core}, device_id_type=MESH)
    pl.semaphore_signal(barrier, inc=1, device_id={"term": other_chip}, device_id_type=MESH)

    @pl.when(has_up)
    def _():
        pl.semaphore_signal(barrier, inc=1, device_id={"sec": sec + 2}, device_id_type=MESH)

    @pl.when(has_down)
    def _():
        pl.semaphore_signal(barrier, inc=1, device_id={"sec": sec - 2}, device_id_type=MESH)

    pl.semaphore_wait(barrier, 3 + has_up.astype(jnp.int32) + has_down.astype(jnp.int32))

    push_own(0)
    locals_ = (
        pltpu.make_async_copy(psi_h, psi_v, local_sem.at[0]),
        pltpu.make_async_copy(right_h, window(0, sec), local_sem.at[1]),
        pltpu.make_async_copy(left_h, window(1, sec), local_sem.at[2]),
    )
    for copy in locals_:
        copy.start()

    @pl.loop(1, line)
    def _(step):
        forward(0, step)

    push_own(1)
    for copy in locals_:
        copy.wait()

    @pl.loop(0, line)
    def _(place):
        await_slot(0, slot_of(place, 1 - side))

    forward(1, 1)

    @pl.loop(0, tiles)
    def _(k):
        moved = psi_v[lax.rem(sources[0, k], tiles)]
        chosen = right_v[sectors[k, 1]]
        half_v[k] = jnp.dot(moved, chosen, preferred_element_type=jnp.float32).astype(jnp.bfloat16)

    def apply_left(block):
        owner = block // per_owner
        owner_core = lax.rem(owner, 2)
        owner_chip = owner // 2
        await_slot(1, slot_of(block, 1 - side))

        @pl.loop(0, left_v.shape[0])
        def _(i):
            left_now[i] = left_v[i, block_rows(block), :]

        @pl.loop(0, GROUPS)
        def _(group):
            @pl.loop(0, size // 2)
            def _(i):
                for j in range(2):
                    k = group * size + i * 2 + j
                    chosen = left_now[sectors[k, 0]]
                    psi_v[k, block_rows(block), :] = jnp.dot(
                        chosen, half_v[k], preferred_element_type=jnp.float32
                    ).astype(jnp.bfloat16)

            @pl.when(core != owner_core)
            def _():
                core_copy(block, group).start()

        @pl.when((core == owner_core) & (chip != owner_chip))
        def _():
            slot = owner_chip * per_owner + lax.rem(block, per_owner)

            @pl.loop(0, GROUPS)
            def _(group):
                core_copy(block, group).wait_recv()

                @pl.loop(0, size)
                def _(i):
                    k = group * size + i
                    psi_v[k, block_rows(block), :] = (
                        psi_v[k, block_rows(block), :].astype(jnp.float32)
                        + core_in[slot, k].astype(jnp.float32)
                    ).astype(jnp.bfloat16)

                chip_copy(block, group).start()

    @pl.loop(0, line)
    def _(step):
        @pl.when(step > 1)
        def _():
            forward(1, step)

        @pl.when(spot - step >= 0)
        def _():
            apply_left(spot - step)

        @pl.when((step > 0) & (spot + step < line))
        def _():
            apply_left(spot + step)

    def out_copy(j, group):
        block = term * per_owner + j
        return pltpu.make_async_copy(
            psi_v.at[group_rows(group), block_rows(block), :],
            out_h.at[group_rows(group), pl.ds(pl.multiple_of(j * wide, wide), wide), :],
            out_sem.at[j, group],
        )

    @pl.loop(0, per_owner)
    def _(j):
        block = term * per_owner + j

        @pl.loop(0, GROUPS)
        def _(group):
            core_copy(block, group).wait_recv()
            chip_copy(block, group).wait_recv()

            @pl.loop(0, size)
            def _(i):
                k = group * size + i
                psi_v[k, block_rows(block), :] = (
                    psi_v[k, block_rows(block), :].astype(jnp.float32)
                    + core_in[chip * per_owner + j, k].astype(jnp.float32)
                    + chip_in[j, k].astype(jnp.float32)
                ).astype(jnp.bfloat16)

            out_copy(j, group).start()

    @pl.loop(0, line)
    def _(place):
        for kind in range(2):
            to_pair(kind, place, owned[kind]).wait_send()

            @pl.when(has_up & (place <= spot))
            def _():
                to_up(kind, place, owned[kind]).wait_send()

            @pl.when(has_down & (place >= spot))
            def _():
                to_down(kind, place, owned[kind]).wait_send()

        owner = place // per_owner

        @pl.loop(0, GROUPS)
        def _(group):
            @pl.when(core != lax.rem(owner, 2))
            def _():
                core_copy(place, group).wait_send()

            @pl.when((core == lax.rem(owner, 2)) & (chip != owner // 2))
            def _():
                chip_copy(place, group).wait_send()

    @pl.loop(0, per_owner)
    def _(j):
        @pl.loop(0, GROUPS)
        def _(group):
            out_copy(j, group).wait()


def body(psi_tiles, sectors, sources, left_env, right_env):
    n = lax.axis_size("sec")
    terms = lax.axis_size("term")
    tiles, width, _ = psi_tiles.shape
    nsec = left_env.shape[1]
    line = n // 2
    wide = 2 * width // n
    kind = jnp.bfloat16
    dma = pltpu.SemaphoreType.DMA
    return pl.pallas_call(
        functools.partial(kernel, n, terms),
        out_shape=jax.ShapeDtypeStruct((tiles, width // terms, width), kind),
        in_specs=[pl.BlockSpec(memory_space=pltpu.SMEM)] * 2 + [pl.BlockSpec(memory_space=pl.ANY)] * 3,
        out_specs=pl.BlockSpec(memory_space=pl.ANY),
        scratch_shapes=[
            pltpu.VMEM((tiles, width, width), kind),
            pltpu.VMEM((nsec, width, width), kind),
            pltpu.VMEM((nsec, width, width), kind),
            pltpu.VMEM((nsec, wide, width), kind),
            pltpu.VMEM((tiles, width, width), kind),
            pltpu.VMEM((line // 2, tiles, wide, width), kind),
            pltpu.VMEM((line // terms, tiles, wide, width), kind),
            dma((3,)),
            dma((2, n)),
            dma((2, line)),
            dma((2, line)),
            dma((2, line)),
            dma((line, GROUPS)),
            dma((line, GROUPS)),
            dma((line, GROUPS)),
            dma((line, GROUPS)),
            dma((line // terms, GROUPS)),
        ],
        compiler_params=pltpu.CompilerParams(
            collective_id=0, has_side_effects=True, vmem_limit_bytes=60 * 1024 * 1024
        ),
        cost_estimate=pl.CostEstimate(
            flops=4 * tiles * width**3,
            bytes_accessed=2 * (tiles * width * width + 2 * nsec * width * width),
            transcendentals=0,
        ),
    )(sectors, sources, psi_tiles, left_env[0], right_env[0])


def solution(mesh):
    placed = (
        P("sec", None, None),
        P("sec", None),
        P("term", "sec"),
        P("term", None, "sec", None),
        P("term", None, "sec", None),
    )
    return jax.shard_map(
        body, mesh=mesh, in_specs=placed, out_specs=P("sec", "term", None), check_vma=False
    )
```

```python
import functools

import jax
import jax.numpy as jnp
from jax import lax
from jax.experimental import pallas as pl
from jax.experimental.pallas import tpu as pltpu
from jax.sharding import PartitionSpec as P

MESH = pl.DeviceIdType.MESH
GROUPS = 4


def kernel(
    n,
    terms,
    sectors,
    sources,
    psi_h,
    left_h,
    right_h,
    out_h,
    psi_v,
    right_v,
    left_v,
    left_now,
    half_v,
    core_in,
    chip_in,
    local_sem,
    recv_sem,
    pair_sem,
    up_sem,
    down_sem,
    mate_sem,
    core_send,
    core_recv,
    chip_send,
    chip_recv,
    out_sem,
):
    tiles = psi_h.shape[0]
    rows = right_h.shape[1]
    line = n // 2
    wide = 2 * rows
    per_owner = line // terms
    size = tiles // GROUPS
    term = lax.axis_index("term")
    sec = lax.axis_index("sec")
    core = lax.rem(term, 2)
    chip = term // 2
    spot = sec // 2
    side = lax.rem(sec, 2)
    pair = spot * 2 + 1 - side
    other_core = chip * 2 + 1 - core
    other_chip = (1 - chip) * 2 + core
    has_up = spot + 1 < line
    has_down = spot > 0
    mate = spot + 1 - 2 * lax.rem(spot, 2)
    gathered = (right_v, left_v)
    owned = (right_h, left_h)

    def slot_of(place, parity):
        return place * 2 + parity

    def window(kind, slot):
        return gathered[kind].at[:, pl.ds(pl.multiple_of(slot * rows, rows), rows), :]

    def env_copy(kind, slot, src, target, sem):
        return pltpu.make_async_remote_copy(
            src_ref=src,
            dst_ref=window(kind, slot),
            send_sem=sem,
            recv_sem=recv_sem.at[kind, slot],
            device_id={"sec": target},
            device_id_type=MESH,
        )

    def to_pair(kind, place, src):
        return env_copy(kind, slot_of(place, side), src, pair, pair_sem.at[kind, place])

    def to_up(kind, place, src):
        return env_copy(kind, slot_of(place, side), src, sec + 2, up_sem.at[kind, place])

    def to_down(kind, place, src):
        return env_copy(kind, slot_of(place, side), src, sec - 2, down_sem.at[kind, place])

    def to_mate(kind):
        slot = slot_of(spot, 1 - side)
        return env_copy(kind, slot, window(kind, slot), mate * 2 + side, mate_sem.at[kind])

    def await_slot(kind, slot):
        env_copy(kind, slot, owned[kind], pair, pair_sem.at[kind, 0]).wait_recv()

    def push_own(kind):
        @pl.when(has_down)
        def _():
            to_down(kind, spot, owned[kind]).start()

        @pl.when(has_up)
        def _():
            to_up(kind, spot, owned[kind]).start()

        to_pair(kind, spot, owned[kind]).start()

    def send_pair(kind, place, slot):
        if kind == 0:
            to_pair(kind, place, window(kind, slot)).start()
        else:

            @pl.when(place != mate)
            def _():
                to_pair(kind, place, window(kind, slot)).start()

    def forward(kind, step):
        @pl.when(spot - step >= 0)
        def _():
            place = spot - step
            slot = slot_of(place, side)
            await_slot(kind, slot)

            @pl.when(has_up)
            def _():
                to_up(kind, place, window(kind, slot)).start()

            send_pair(kind, place, slot)

        @pl.when(spot + step < line)
        def _():
            place = spot + step
            slot = slot_of(place, side)
            await_slot(kind, slot)

            @pl.when(has_down)
            def _():
                to_down(kind, place, window(kind, slot)).start()

            send_pair(kind, place, slot)

    def block_rows(block):
        return pl.ds(pl.multiple_of(block * wide, wide), wide)

    def group_rows(group):
        return pl.ds(group * size, size)

    def core_copy(block, group):
        owner = block // per_owner
        slot = (owner // 2) * per_owner + lax.rem(block, per_owner)
        return pltpu.make_async_remote_copy(
            src_ref=psi_v.at[group_rows(group), block_rows(block), :],
            dst_ref=core_in.at[slot, group_rows(group)],
            send_sem=core_send.at[block, group],
            recv_sem=core_recv.at[block, group],
            device_id={"term": other_core},
            device_id_type=MESH,
        )

    def chip_copy(block, group):
        return pltpu.make_async_remote_copy(
            src_ref=psi_v.at[group_rows(group), block_rows(block), :],
            dst_ref=chip_in.at[lax.rem(block, per_owner), group_rows(group)],
            send_sem=chip_send.at[block, group],
            recv_sem=chip_recv.at[block, group],
            device_id={"term": other_chip},
            device_id_type=MESH,
        )

    barrier = pltpu.get_barrier_semaphore()
    pl.semaphore_signal(barrier, inc=1, device_id={"sec": pair}, device_id_type=MESH)
    pl.semaphore_signal(barrier, inc=1, device_id={"term": other_core}, device_id_type=MESH)
    pl.semaphore_signal(barrier, inc=1, device_id={"term": other_chip}, device_id_type=MESH)

    @pl.when(has_up)
    def _():
        pl.semaphore_signal(barrier, inc=1, device_id={"sec": sec + 2}, device_id_type=MESH)

    @pl.when(has_down)
    def _():
        pl.semaphore_signal(barrier, inc=1, device_id={"sec": sec - 2}, device_id_type=MESH)

    pl.semaphore_wait(barrier, 3 + has_up.astype(jnp.int32) + has_down.astype(jnp.int32))

    push_own(0)
    locals_ = (
        pltpu.make_async_copy(psi_h, psi_v, local_sem.at[0]),
        pltpu.make_async_copy(right_h, window(0, sec), local_sem.at[1]),
        pltpu.make_async_copy(left_h, window(1, sec), local_sem.at[2]),
    )
    for copy in locals_:
        copy.start()

    @pl.loop(1, line)
    def _(step):
        forward(0, step)

    push_own(1)
    for copy in locals_:
        copy.wait()

    @pl.loop(0, line)
    def _(place):
        await_slot(0, slot_of(place, 1 - side))

    forward(1, 1)

    @pl.loop(0, tiles)
    def _(k):
        moved = psi_v[lax.rem(sources[0, k], tiles)]
        chosen = right_v[sectors[k, 1]]
        half_v[k] = jnp.dot(moved, chosen, preferred_element_type=jnp.float32).astype(jnp.bfloat16)

    def apply_left(block):
        owner = block // per_owner
        owner_core = lax.rem(owner, 2)
        owner_chip = owner // 2
        await_slot(1, slot_of(block, 1 - side))

        @pl.when(block == spot)
        def _():
            to_mate(1).start()

        @pl.loop(0, left_v.shape[0])
        def _(i):
            left_now[i] = left_v[i, block_rows(block), :]

        @pl.loop(0, GROUPS)
        def _(group):
            @pl.loop(0, size // 2)
            def _(i):
                for j in range(2):
                    k = group * size + i * 2 + j
                    chosen = left_now[sectors[k, 0]]
                    psi_v[k, block_rows(block), :] = jnp.dot(
                        chosen, half_v[k], preferred_element_type=jnp.float32
                    ).astype(jnp.bfloat16)

            @pl.when(core != owner_core)
            def _():
                core_copy(block, group).start()

        @pl.when((core == owner_core) & (chip != owner_chip))
        def _():
            slot = owner_chip * per_owner + lax.rem(block, per_owner)

            @pl.loop(0, GROUPS)
            def _(group):
                core_copy(block, group).wait_recv()

                @pl.loop(0, size)
                def _(i):
                    k = group * size + i
                    psi_v[k, block_rows(block), :] = (
                        psi_v[k, block_rows(block), :].astype(jnp.float32)
                        + core_in[slot, k].astype(jnp.float32)
                    ).astype(jnp.bfloat16)

                chip_copy(block, group).start()

    @pl.loop(0, line)
    def _(step):
        @pl.when(step > 1)
        def _():
            forward(1, step)

        @pl.when(spot - step >= 0)
        def _():
            apply_left(spot - step)

        @pl.when((step > 0) & (spot + step < line))
        def _():
            apply_left(spot + step)

    def out_copy(j, group):
        block = term * per_owner + j
        return pltpu.make_async_copy(
            psi_v.at[group_rows(group), block_rows(block), :],
            out_h.at[group_rows(group), pl.ds(pl.multiple_of(j * wide, wide), wide), :],
            out_sem.at[j, group],
        )

    @pl.loop(0, per_owner)
    def _(j):
        block = term * per_owner + j

        @pl.loop(0, GROUPS)
        def _(group):
            core_copy(block, group).wait_recv()
            chip_copy(block, group).wait_recv()

            @pl.loop(0, size)
            def _(i):
                k = group * size + i
                psi_v[k, block_rows(block), :] = (
                    psi_v[k, block_rows(block), :].astype(jnp.float32)
                    + core_in[chip * per_owner + j, k].astype(jnp.float32)
                    + chip_in[j, k].astype(jnp.float32)
                ).astype(jnp.bfloat16)

            out_copy(j, group).start()

    to_mate(1).wait_send()

    @pl.loop(0, line)
    def _(place):
        to_pair(0, place, owned[0]).wait_send()

        @pl.when(place != mate)
        def _():
            to_pair(1, place, owned[1]).wait_send()

        for kind in range(2):

            @pl.when(has_up & (place <= spot))
            def _():
                to_up(kind, place, owned[kind]).wait_send()

            @pl.when(has_down & (place >= spot))
            def _():
                to_down(kind, place, owned[kind]).wait_send()

        owner = place // per_owner

        @pl.loop(0, GROUPS)
        def _(group):
            @pl.when(core != lax.rem(owner, 2))
            def _():
                core_copy(place, group).wait_send()

            @pl.when((core == lax.rem(owner, 2)) & (chip != owner // 2))
            def _():
                chip_copy(place, group).wait_send()

    @pl.loop(0, per_owner)
    def _(j):
        @pl.loop(0, GROUPS)
        def _(group):
            out_copy(j, group).wait()


def body(psi_tiles, sectors, sources, left_env, right_env):
    n = lax.axis_size("sec")
    terms = lax.axis_size("term")
    tiles, width, _ = psi_tiles.shape
    nsec = left_env.shape[1]
    line = n // 2
    wide = 2 * width // n
    kind = jnp.bfloat16
    dma = pltpu.SemaphoreType.DMA
    return pl.pallas_call(
        functools.partial(kernel, n, terms),
        out_shape=jax.ShapeDtypeStruct((tiles, width // terms, width), kind),
        in_specs=[pl.BlockSpec(memory_space=pltpu.SMEM)] * 2 + [pl.BlockSpec(memory_space=pl.ANY)] * 3,
        out_specs=pl.BlockSpec(memory_space=pl.ANY),
        scratch_shapes=[
            pltpu.VMEM((tiles, width, width), kind),
            pltpu.VMEM((nsec, width, width), kind),
            pltpu.VMEM((nsec, width, width), kind),
            pltpu.VMEM((nsec, wide, width), kind),
            pltpu.VMEM((tiles, width, width), kind),
            pltpu.VMEM((line // 2, tiles, wide, width), kind),
            pltpu.VMEM((line // terms, tiles, wide, width), kind),
            dma((3,)),
            dma((2, n)),
            dma((2, line)),
            dma((2, line)),
            dma((2, line)),
            dma((2,)),
            dma((line, GROUPS)),
            dma((line, GROUPS)),
            dma((line, GROUPS)),
            dma((line, GROUPS)),
            dma((line // terms, GROUPS)),
        ],
        compiler_params=pltpu.CompilerParams(
            collective_id=0, has_side_effects=True, vmem_limit_bytes=60 * 1024 * 1024
        ),
        cost_estimate=pl.CostEstimate(
            flops=4 * tiles * width**3,
            bytes_accessed=2 * (tiles * width * width + 2 * nsec * width * width),
            transcendentals=0,
        ),
    )(sectors, sources, psi_tiles, left_env[0], right_env[0])


def solution(mesh):
    placed = (
        P("sec", None, None),
        P("sec", None),
        P("term", "sec"),
        P("term", None, "sec", None),
        P("term", None, "sec", None),
    )
    return jax.shard_map(
        body, mesh=mesh, in_specs=placed, out_specs=P("sec", "term", None), check_vma=False
    )
```

```python
import functools

import jax
import jax.numpy as jnp
from jax import lax
from jax.experimental import pallas as pl
from jax.experimental.pallas import tpu as pltpu
from jax.sharding import PartitionSpec as P

MESH = pl.DeviceIdType.MESH
GROUPS = 4


def halves_of(rows):
    return 2 if rows % 32 == 0 else 1


def kernel(
    n,
    terms,
    sectors,
    sources,
    psi_h,
    left_h,
    right_h,
    out_h,
    psi_v,
    right_v,
    left_v,
    left_now,
    half_v,
    core_in,
    chip_in,
    local_sem,
    recv_sem,
    pair_sem,
    up_sem,
    down_sem,
    mate_sem,
    core_send,
    core_recv,
    chip_send,
    chip_recv,
    out_sem,
):
    tiles = psi_h.shape[0]
    rows = right_h.shape[1]
    line = n // 2
    halves = halves_of(rows)
    part = rows // halves
    wide = 2 * part
    units = line * halves
    per_owner = units // terms
    size = tiles // GROUPS
    term = lax.axis_index("term")
    sec = lax.axis_index("sec")
    core = lax.rem(term, 2)
    chip = term // 2
    spot = sec // 2
    side = lax.rem(sec, 2)
    pair = spot * 2 + 1 - side
    other_core = chip * 2 + 1 - core
    other_chip = (1 - chip) * 2 + core
    has_up = spot + 1 < line
    has_down = spot > 0
    mate = spot + 1 - 2 * lax.rem(spot, 2)
    kinds = range(1, 1 + halves)
    owned = [right_h] + [left_h.at[:, pl.ds(h * part, part), :] for h in range(halves)]

    def slot_of(place, parity):
        return place * 2 + parity

    def window(kind, slot):
        if kind == 0:
            return right_v.at[:, pl.ds(pl.multiple_of(slot * rows, rows), rows), :]
        return left_v.at[:, pl.ds(pl.multiple_of(slot * rows + (kind - 1) * part, part), part), :]

    def env_copy(kind, slot, src, target, sem):
        return pltpu.make_async_remote_copy(
            src_ref=src,
            dst_ref=window(kind, slot),
            send_sem=sem,
            recv_sem=recv_sem.at[kind, slot],
            device_id={"sec": target},
            device_id_type=MESH,
        )

    def to_pair(kind, place, src):
        return env_copy(kind, slot_of(place, side), src, pair, pair_sem.at[kind, place])

    def to_up(kind, place, src):
        return env_copy(kind, slot_of(place, side), src, sec + 2, up_sem.at[kind, place])

    def to_down(kind, place, src):
        return env_copy(kind, slot_of(place, side), src, sec - 2, down_sem.at[kind, place])

    def to_mate(kind):
        slot = slot_of(spot, 1 - side)
        return env_copy(kind, slot, window(kind, slot), mate * 2 + side, mate_sem.at[kind])

    def await_slot(kind, slot):
        env_copy(kind, slot, owned[kind], pair, pair_sem.at[kind, 0]).wait_recv()

    def push_own(kind):
        @pl.when(has_down)
        def _():
            to_down(kind, spot, owned[kind]).start()

        @pl.when(has_up)
        def _():
            to_up(kind, spot, owned[kind]).start()

        to_pair(kind, spot, owned[kind]).start()

    def send_pair(kind, place, slot):
        if kind == 0:
            to_pair(kind, place, window(kind, slot)).start()
        else:

            @pl.when(place != mate)
            def _():
                to_pair(kind, place, window(kind, slot)).start()

    def forward(kind, step):
        @pl.when(spot - step >= 0)
        def _():
            place = spot - step
            slot = slot_of(place, side)
            await_slot(kind, slot)

            @pl.when(has_up)
            def _():
                to_up(kind, place, window(kind, slot)).start()

            send_pair(kind, place, slot)

        @pl.when(spot + step < line)
        def _():
            place = spot + step
            slot = slot_of(place, side)
            await_slot(kind, slot)

            @pl.when(has_down)
            def _():
                to_down(kind, place, window(kind, slot)).start()

            send_pair(kind, place, slot)

    def block_rows(block):
        return pl.ds(pl.multiple_of(block * wide, wide), wide)

    def group_rows(group):
        return pl.ds(group * size, size)

    def core_copy(block, group):
        owner = block // per_owner
        slot = (owner // 2) * per_owner + lax.rem(block, per_owner)
        return pltpu.make_async_remote_copy(
            src_ref=psi_v.at[group_rows(group), block_rows(block), :],
            dst_ref=core_in.at[slot, group_rows(group)],
            send_sem=core_send.at[block, group],
            recv_sem=core_recv.at[block, group],
            device_id={"term": other_core},
            device_id_type=MESH,
        )

    def chip_copy(block, group):
        return pltpu.make_async_remote_copy(
            src_ref=psi_v.at[group_rows(group), block_rows(block), :],
            dst_ref=chip_in.at[lax.rem(block, per_owner), group_rows(group)],
            send_sem=chip_send.at[block, group],
            recv_sem=chip_recv.at[block, group],
            device_id={"term": other_chip},
            device_id_type=MESH,
        )

    barrier = pltpu.get_barrier_semaphore()
    pl.semaphore_signal(barrier, inc=1, device_id={"sec": pair}, device_id_type=MESH)
    pl.semaphore_signal(barrier, inc=1, device_id={"term": other_core}, device_id_type=MESH)
    pl.semaphore_signal(barrier, inc=1, device_id={"term": other_chip}, device_id_type=MESH)

    @pl.when(has_up)
    def _():
        pl.semaphore_signal(barrier, inc=1, device_id={"sec": sec + 2}, device_id_type=MESH)

    @pl.when(has_down)
    def _():
        pl.semaphore_signal(barrier, inc=1, device_id={"sec": sec - 2}, device_id_type=MESH)

    pl.semaphore_wait(barrier, 3 + has_up.astype(jnp.int32) + has_down.astype(jnp.int32))

    push_own(0)
    locals_ = (
        pltpu.make_async_copy(psi_h, psi_v, local_sem.at[0]),
        pltpu.make_async_copy(right_h, window(0, sec), local_sem.at[1]),
        pltpu.make_async_copy(
            left_h, left_v.at[:, pl.ds(pl.multiple_of(sec * rows, rows), rows), :], local_sem.at[2]
        ),
    )
    for copy in locals_:
        copy.start()

    @pl.loop(1, line)
    def _(step):
        forward(0, step)

    push_own(1)
    for copy in locals_:
        copy.wait()

    @pl.loop(0, line)
    def _(place):
        await_slot(0, slot_of(place, 1 - side))

    forward(1, 1)

    @pl.loop(0, tiles)
    def _(k):
        moved = psi_v[lax.rem(sources[0, k], tiles)]
        chosen = right_v[sectors[k, 1]]
        half_v[k] = jnp.dot(moved, chosen, preferred_element_type=jnp.float32).astype(jnp.bfloat16)

    def apply_left(place, kind):
        block = place * halves + kind - 1
        owner = block // per_owner
        owner_core = lax.rem(owner, 2)
        owner_chip = owner // 2
        await_slot(kind, slot_of(place, 1 - side))

        @pl.when(place == spot)
        def _():
            to_mate(kind).start()

        @pl.loop(0, left_v.shape[0])
        def _(i):
            for parity in range(2):
                start = pl.multiple_of((place * 2 + parity) * rows + (kind - 1) * part, part)
                left_now[i, parity * part : (parity + 1) * part] = left_v[i, pl.ds(start, part), :]

        @pl.loop(0, GROUPS)
        def _(group):
            @pl.loop(0, size // 2)
            def _(i):
                for j in range(2):
                    k = group * size + i * 2 + j
                    chosen = left_now[sectors[k, 0]]
                    psi_v[k, block_rows(block), :] = jnp.dot(
                        chosen, half_v[k], preferred_element_type=jnp.float32
                    ).astype(jnp.bfloat16)

            @pl.when(core != owner_core)
            def _():
                core_copy(block, group).start()

        @pl.when((core == owner_core) & (chip != owner_chip))
        def _():
            slot = owner_chip * per_owner + lax.rem(block, per_owner)

            @pl.loop(0, GROUPS)
            def _(group):
                core_copy(block, group).wait_recv()

                @pl.loop(0, size)
                def _(i):
                    k = group * size + i
                    psi_v[k, block_rows(block), :] = (
                        psi_v[k, block_rows(block), :].astype(jnp.float32)
                        + core_in[slot, k].astype(jnp.float32)
                    ).astype(jnp.bfloat16)

                chip_copy(block, group).start()

    for kind in kinds:
        if kind > 1:
            forward(kind, 1)

        @pl.loop(0, line)
        def _(step):
            @pl.when(step > 1)
            def _():
                forward(kind, step)

            if kind < halves:

                @pl.when(step == line - 2)
                def _():
                    push_own(kind + 1)

            @pl.when(spot - step >= 0)
            def _():
                apply_left(spot - step, kind)

            @pl.when((step > 0) & (spot + step < line))
            def _():
                apply_left(spot + step, kind)

    def out_copy(j, group, parity):
        start = (term * per_owner + j) * wide + parity * part
        target = (j // halves) * 2 * rows + parity * rows + lax.rem(j, halves) * part
        return pltpu.make_async_copy(
            psi_v.at[group_rows(group), pl.ds(pl.multiple_of(start, part), part), :],
            out_h.at[group_rows(group), pl.ds(pl.multiple_of(target, part), part), :],
            out_sem.at[j, group, parity],
        )

    @pl.loop(0, per_owner)
    def _(j):
        block = term * per_owner + j

        @pl.loop(0, GROUPS)
        def _(group):
            core_copy(block, group).wait_recv()
            chip_copy(block, group).wait_recv()

            @pl.loop(0, size)
            def _(i):
                k = group * size + i
                psi_v[k, block_rows(block), :] = (
                    psi_v[k, block_rows(block), :].astype(jnp.float32)
                    + core_in[chip * per_owner + j, k].astype(jnp.float32)
                    + chip_in[j, k].astype(jnp.float32)
                ).astype(jnp.bfloat16)

            for parity in range(2):
                out_copy(j, group, parity).start()

    for kind in kinds:
        to_mate(kind).wait_send()

    @pl.loop(0, line)
    def _(place):
        to_pair(0, place, owned[0]).wait_send()

        @pl.when(place != mate)
        def _():
            for kind in kinds:
                to_pair(kind, place, owned[kind]).wait_send()

        for kind in range(1 + halves):

            @pl.when(has_up & (place <= spot))
            def _():
                to_up(kind, place, owned[kind]).wait_send()

            @pl.when(has_down & (place >= spot))
            def _():
                to_down(kind, place, owned[kind]).wait_send()

    @pl.loop(0, units)
    def _(place):
        owner = place // per_owner

        @pl.loop(0, GROUPS)
        def _(group):
            @pl.when(core != lax.rem(owner, 2))
            def _():
                core_copy(place, group).wait_send()

            @pl.when((core == lax.rem(owner, 2)) & (chip != owner // 2))
            def _():
                chip_copy(place, group).wait_send()

    @pl.loop(0, per_owner)
    def _(j):
        @pl.loop(0, GROUPS)
        def _(group):
            for parity in range(2):
                out_copy(j, group, parity).wait()


def body(psi_tiles, sectors, sources, left_env, right_env):
    n = lax.axis_size("sec")
    terms = lax.axis_size("term")
    tiles, width, _ = psi_tiles.shape
    nsec = left_env.shape[1]
    line = n // 2
    halves = halves_of(width // n)
    wide = 2 * width // n // halves
    units = line * halves
    kind = jnp.bfloat16
    dma = pltpu.SemaphoreType.DMA
    return pl.pallas_call(
        functools.partial(kernel, n, terms),
        out_shape=jax.ShapeDtypeStruct((tiles, width // terms, width), kind),
        in_specs=[pl.BlockSpec(memory_space=pltpu.SMEM)] * 2 + [pl.BlockSpec(memory_space=pl.ANY)] * 3,
        out_specs=pl.BlockSpec(memory_space=pl.ANY),
        scratch_shapes=[
            pltpu.VMEM((tiles, width, width), kind),
            pltpu.VMEM((nsec, width, width), kind),
            pltpu.VMEM((nsec, width, width), kind),
            pltpu.VMEM((nsec, wide, width), kind),
            pltpu.VMEM((tiles, width, width), kind),
            pltpu.VMEM((units // 2, tiles, wide, width), kind),
            pltpu.VMEM((units // terms, tiles, wide, width), kind),
            dma((3,)),
            dma((1 + halves, n)),
            dma((1 + halves, line)),
            dma((1 + halves, line)),
            dma((1 + halves, line)),
            dma((1 + halves,)),
            dma((units, GROUPS)),
            dma((units, GROUPS)),
            dma((units, GROUPS)),
            dma((units, GROUPS)),
            dma((units // terms, GROUPS, 2)),
        ],
        compiler_params=pltpu.CompilerParams(
            collective_id=0, has_side_effects=True, vmem_limit_bytes=60 * 1024 * 1024
        ),
        cost_estimate=pl.CostEstimate(
            flops=4 * tiles * width**3,
            bytes_accessed=2 * (tiles * width * width + 2 * nsec * width * width),
            transcendentals=0,
        ),
    )(sectors, sources, psi_tiles, left_env[0], right_env[0])


def solution(mesh):
    placed = (
        P("sec", None, None),
        P("sec", None),
        P("term", "sec"),
        P("term", None, "sec", None),
        P("term", None, "sec", None),
    )
    return jax.shard_map(
        body, mesh=mesh, in_specs=placed, out_specs=P("sec", "term", None), check_vma=False
    )
```
